128 devices in a mesh: dp: 32 (over x_hi, y, z), tensor: 4 (over x_lo, core).
Axes of the slice: x: 4 (x_hi: 2, x_lo: 2; x = x_hi * 2 + x_lo), y: 4, z: 4, core: 2. Of those that a mesh axis runs over, the one named last changes fastest.
Arguments:
- tokens: bfloat16 [2, 32, 256, 2048], P(None, 'dp', 'tensor'), may hold values from -6 to 6
- cotangent: bfloat16 [2, 32, 256, 2048], P(None, 'dp', 'tensor'), may hold values from -6 to 6
- lengths: int32 [2, 32], P(None, 'dp'), may hold values from 64 to 256, as said below
- in_weight: bfloat16 [1, 2048, 6144], P(None, ('dp', 'tensor')), may hold values from -0.125 to 0.125
- out_weight: bfloat16 [1, 2048, 2048], P(None, ('dp', 'tensor')), may hold values from -0.125 to 0.125
- norm_gains: bfloat16 [1, 2048, 3], P(None, ('dp', 'tensor')), may hold values from 0.5 to 1.5
- forget_bias: bfloat16 [1, 2048], P(None, ('dp', 'tensor')), may hold values from -1 to 8
- gate_weight: bfloat16 [1, 2048, 5632], P(None, 'dp', 'tensor'), may hold values from -0.125 to 0.125
- up_weight: bfloat16 [1, 2048, 5632], P(None, 'dp', 'tensor'), may hold values from -0.125 to 0.125
- down_weight: bfloat16 [1, 2048, 5632], P(None, 'dp', 'tensor'), may hold values from -0.078125 to 0.078125
Outputs:
- activations: float32 [2, 32, 256, 2048], P(None, 'dp', 'tensor')
- token_grad: float32 [2, 32, 256, 2048], P(None, 'dp', 'tensor')
- in_weight_grad: float32 [1, 2048, 6144], P(None, ('dp', 'tensor'))
- out_weight_grad: float32 [1, 2048, 2048], P(None, ('dp', 'tensor'))
- gains_grad: float32 [1, 2048, 3], P(None, ('dp', 'tensor'))
- bias_grad: float32 [1, 2048], P(None, ('dp', 'tensor'))
- gate_grad: float32 [1, 2048, 5632], P(None, 'dp', 'tensor')
- up_grad: float32 [1, 2048, 5632], P(None, 'dp', 'tensor')
- down_grad: float32 [1, 2048, 5632], P(None, 'dp', 'tensor')
The draws below stay inside these ranges and needn't reach their ends.
Inputs may be any that keep to these rules, and one draw needn't show every extreme that they name: `lengths`: in every micro-batch one sequence, chosen by the seed, has all 256 tokens valid.
All inputs are finite; a program needn't handle non-finite values.
Results may differ from the reference program's by a relative error of at most 0.024.
The reference program's roundings to bfloat16 on the way count: a program that leaves them out, or rounds other values in their place, can miss the bound.
Values may be sent and summed in bfloat16 or wider, within the bound.
No kernel may reach another device: no remote copies, remote signals or barrier semaphores. Data moves between devices by JAX's collectives and lax.ppermute only.
A program may use at most 384 MiB of HBM per device.

```python
import jax
import jax.numpy as jnp
from jax import lax

D = 2048
FF = 5632
SEQ = 256
MICRO = 2
LAYERS = 1
SEQS = 32


def draw_lengths(key, part):
    key = jax.random.fold_in(key, 7)
    first_key, second_key = jax.random.split(key)
    spans = jax.random.randint(first_key, (MICRO, SEQS), SEQ // 4, SEQ + 1)
    chosen = jax.random.randint(second_key, (MICRO, 1), 0, SEQS)
    column = jnp.arange(SEQS)[None, :]
    return jnp.where(column == chosen, SEQ, spans).astype(jnp.int32)


def block_scale(rng, extent, cuts, least, high):
    def one(dim, shards_of):
        draws = jax.random.uniform(jax.random.fold_in(jax.random.fold_in(rng, 6), dim), (shards_of,), jnp.float32, least / len(cuts), high / len(cuts))
        return jnp.repeat(jnp.exp(draws), extent[dim] // shards_of).reshape((-1,) + (1,) * (len(extent) - dim - 1))

    gain = one(*cuts[0])
    for cut in cuts[1:]:
        gain = gain * one(*cut)
    return gain


def gaussian(key, extent, deviation, reach, pieces=(), held_as=jnp.bfloat16):
    array = deviation * jax.random.normal(key, extent, jnp.float32)
    if pieces:
        array = array * block_scale(key, extent, pieces, -0.22, 0.18)
    return jnp.clip(array, -reach, reach).astype(held_as)


def setup_inputs(seed: int = 0) -> dict:
    arg_keys = jax.random.split(jax.random.key(seed), 11)
    tokens = gaussian(arg_keys[0], (MICRO, SEQS, SEQ, D), 1.0, 6.0, ((1, 32), (2, 4)))
    cotangent = gaussian(arg_keys[1], (MICRO, SEQS, SEQ, D), 1.0, 6.0, ((1, 32), (2, 4)))
    lengths = draw_lengths(jax.random.fold_in(arg_keys[10], 71), 0)
    in_weight = gaussian(arg_keys[3], (LAYERS, D, 3 * D), D ** -0.5, 0.125, ((1, 128),))
    out_weight = gaussian(arg_keys[4], (LAYERS, D, D), D ** -0.5, 0.125, ((1, 128),))
    norm_gains = jnp.clip(1.0 + 0.1 * jax.random.normal(arg_keys[5], (LAYERS, D, 3), jnp.float32), 0.5, 1.5).astype(jnp.bfloat16)
    forget_bias = jnp.clip(-1.0 + 9.0 * jax.random.uniform(arg_keys[6], (LAYERS, D), jnp.float32) ** block_scale(arg_keys[6], (LAYERS, D), ((1, 128),), -0.2, 0.2), -1.0, 8.0).astype(jnp.bfloat16)
    gate_weight = gaussian(arg_keys[7], (LAYERS, D, FF), D ** -0.5, 0.125, ((1, 32), (2, 4)))
    up_weight = gaussian(arg_keys[8], (LAYERS, D, FF), D ** -0.5, 0.125, ((1, 32), (2, 4)))
    down_weight = gaussian(arg_keys[9], (LAYERS, D, FF), FF ** -0.5, 0.078125, ((1, 32), (2, 4)))
    return dict(tokens=tokens, cotangent=cotangent, lengths=lengths, in_weight=in_weight, out_weight=out_weight, norm_gains=norm_gains, forget_bias=forget_bias, gate_weight=gate_weight, up_weight=up_weight, down_weight=down_weight)


EPS = 1e-06
bundle_size = 4

@jax.custom_vjp
def low(v):
    return lax.optimization_barrier(v.astype(jnp.bfloat16)).astype(jnp.float32)

@jax.custom_vjp
def low_back(v):
    return v

def low_keep(v):
    return (low(v), None)

def low_pass(kept, grad):
    return (grad,)

def back_keep(v):
    return (v, None)

def back_low(kept, grad):
    return (low(grad),)
low.defvjp(low_keep, low_pass)
low_back.defvjp(back_keep, back_low)

def matmul(left, right):
    return jnp.einsum('gtd,de->gte', left, right, precision=lax.Precision.HIGHEST)

def inverse_rms(values):
    return lax.rsqrt(lax.optimization_barrier(jnp.mean(values * values, axis=-1, keepdims=True)) + EPS)

def recurrence(forget, inputs):

    def advance(state_now, pair):
        forget_now, input_now = pair
        state_now = forget_now * state_now + (1.0 - forget_now) * input_now
        return (state_now, state_now)
    start_state = jnp.zeros((forget.shape[0], forget.shape[2]), jnp.float32)
    moved = (jnp.swapaxes(forget, 0, 1), jnp.swapaxes(inputs, 0, 1))
    unused, states = lax.scan(advance, start_state, moved)
    return jnp.swapaxes(states, 0, 1)

def layer_forward(hidden_in, layer_index, in_weight, out_weight, norm_gains, forget_bias, gate_weight, up_weight, down_weight):
    lower_bound = (layer_index + 1) / (LAYERS + 1)
    model_width = hidden_in.shape[-1]
    normed = low(hidden_in * inverse_rms(hidden_in) * norm_gains[layer_index, :, 0])
    projected = low_back(matmul(normed, in_weight[layer_index]))
    part_input = projected[..., :model_width]
    part_forget = projected[..., model_width:2 * model_width]
    part_gate = projected[..., 2 * model_width:]
    inputs = low(jax.nn.silu(part_input))
    forget = low(lower_bound + (1.0 - lower_bound) * jax.nn.sigmoid(part_forget + forget_bias[layer_index]))
    states = recurrence(forget, inputs)
    gated = low(states * inverse_rms(states) * norm_gains[layer_index, :, 1] * jax.nn.silu(part_gate))
    mixed_sum = hidden_in + low_back(matmul(gated, out_weight[layer_index]))
    normed_two = low(mixed_sum * inverse_rms(mixed_sum) * norm_gains[layer_index, :, 2])
    gate_pre = low_back(matmul(normed_two, gate_weight[layer_index]))
    up_pre = low_back(matmul(normed_two, up_weight[layer_index]))
    hidden = low(jax.nn.silu(gate_pre) * up_pre)
    down_out = jnp.einsum('gtf,df->gtd', hidden, down_weight[layer_index], precision=lax.Precision.HIGHEST)
    return mixed_sum + low_back(down_out)

def forward(hidden_in, in_weight, out_weight, norm_gains, forget_bias, gate_weight, up_weight, down_weight):
    current = hidden_in
    for layer_index in range(LAYERS):
        current = layer_forward(current, layer_index, in_weight, out_weight, norm_gains, forget_bias, gate_weight, up_weight, down_weight)
    return current

def reference(tokens, cotangent, lengths, in_weight, out_weight, norm_gains, forget_bias, gate_weight, up_weight, down_weight):
    weights = tuple((weight_item.astype(jnp.float32) for weight_item in (in_weight, out_weight, norm_gains, forget_bias, gate_weight, up_weight, down_weight)))
    positions = jnp.arange(SEQ).astype(jnp.int32)
    keep = (positions[None, None, :] < lengths[:, :, None]).astype(jnp.float32)
    seeds = cotangent.astype(jnp.float32) * keep[..., None]
    model_width = tokens.shape[-1]
    grouped_tokens = tokens.astype(jnp.float32).reshape(-1, bundle_size, SEQ, model_width)
    grouped_seeds = seeds.reshape(-1, bundle_size, SEQ, model_width)

    def one_bundle(summed, pair):
        bundle_tokens, bundle_seeds = pair
        outputs, pullback = jax.vjp(forward, bundle_tokens, *weights)
        grads = pullback(bundle_seeds)
        summed = tuple((running + update for running, update in zip(summed, grads[1:])))
        return (summed, (outputs, grads[0]))
    starting = tuple((jnp.zeros_like(weight_item) for weight_item in weights))
    summed, (outputs, token_grads) = lax.scan(one_bundle, starting, (grouped_tokens, grouped_seeds))
    full_shape = tokens.shape
    return (outputs.reshape(full_shape), token_grads.reshape(full_shape), summed[0], summed[1], summed[2], summed[3], summed[4], summed[5], summed[6])
```

```python
import functools

import jax
import jax.numpy as jnp
from jax import lax
from jax.experimental import pallas as pl
from jax.experimental.pallas import tpu as pltpu
from jax.sharding import Mesh
from jax.sharding import PartitionSpec as P

EPS = 1e-06
LOWER = 0.5
F32 = jnp.float32
BF16 = jnp.bfloat16
LANES = 128
def cost(flops):
    return pl.CostEstimate(flops=flops, bytes_accessed=flops // 400, transcendentals=0)


NO_COST = pl.CostEstimate(flops=0, bytes_accessed=0, transcendentals=0)
DP = ("xh", "y", "z")
TENSOR = ("xl", "c")
CHIPS = ("xh", "xl")
GROUP = ("xh", "xl", "c")
SWAP = ((0, 1), (1, 0))


def dot(left, right):
    return jnp.dot(left, right, preferred_element_type=F32)


def dot_rows(left, right):
    return lax.dot_general(left, right, (((0,), (0,)), ((), ())), preferred_element_type=F32)


def dot_last(left, right):
    return lax.dot_general(left, right, (((1,), (1,)), ((), ())), preferred_element_type=F32)


def inverse_rms(values):
    return lax.rsqrt(jnp.mean(values * values, axis=-1, keepdims=True) + EPS)


RIGHT = ((0, 1), (1, 2), (2, 3), (3, 0))
LEFT = ((1, 0), (2, 1), (3, 2), (0, 3))
OFFSETS = (0, -1, 1, 2)


PLANE = ("y", "z", "c")


def plane_shift(first, step):
    pairs = []
    for y in range(4):
        for z in range(4):
            for c in range(2):
                along_y = (c == 0) == (first == "y")
                to = ((y + step) % 4, z) if along_y else (y, (z + step) % 4)
                pairs.append(((y * 4 + z) * 2 + c, (to[0] * 4 + to[1]) * 2 + c))
    return tuple(pairs)


def to_right(value, axes):
    if axes[0] == PLANE:
        return lax.ppermute(value, PLANE, plane_shift(axes[1], 1))
    return lax.ppermute(value, axes, RIGHT)


def to_left(value, axes):
    if axes[0] == PLANE:
        return lax.ppermute(value, PLANE, plane_shift(axes[1], -1))
    return lax.ppermute(value, axes, LEFT)


def beside(value):
    return lax.ppermute(value, "c", SWAP)


def in_turn(*values):
    return lax.optimization_barrier(values)


def held(value, *earlier):
    return lax.optimization_barrier((value, earlier))[0]


def add_low(left, right):
    return (left.astype(F32) + right.astype(F32)).astype(BF16)


def both_ways(block, axes):
    return to_right(block, axes), to_left(block, axes)


def far_halves(before, behind, axes):
    half = before.shape[0] // 2
    return to_right(before[:half], axes), to_left(behind[half:], axes)


def send_far(top, bottom, axes):
    return to_right(top, axes), to_left(bottom, axes)


def fold(after, before, arrived):
    right = jnp.concatenate([add_low(after[0], arrived[0]), after[1]], axis=0)
    left = jnp.concatenate([before[0], add_low(before[1], arrived[1])], axis=0)
    return right, left


def send_near(right, left, axes):
    return to_right(right, axes), to_left(left, axes)


def total(own, arrived):
    return own.astype(F32) + arrived[0].astype(F32) + arrived[1].astype(F32)


def halved(block):
    half = block.shape[0] // 2
    return block[:half], block[half:]


def sum_kernel(own_ref, *refs):
    others, (top_ref, bottom_ref, *refs) = refs[:-5], refs[-5:]
    rows = refs[0].shape[0]
    each = 4 // len(others)

    def tile(n, _):
        at = pl.ds(pl.multiple_of(n * 16, 16), 16)
        for k, ref in enumerate(refs):
            here = pl.ds(pl.multiple_of(k * rows + n * 16, 16), 16)
            there = pl.ds(pl.multiple_of(k % each * rows + n * 16, 16), 16)
            ref[at, :] = add_low(own_ref[here, :], others[k // each][there, :])
        return _

    lax.fori_loop(0, rows // 16, tile, 0)

    def far_tile(n, _):
        at = pl.ds(pl.multiple_of(n * 16, 16), 16)
        for k, ref in enumerate((top_ref, bottom_ref)):
            here = pl.ds(pl.multiple_of(3 * rows + k * rows // 2 + n * 16, 16), 16)
            there = pl.ds(pl.multiple_of((each - 1) * rows + k * rows // 2 + n * 16, 16), 16)
            ref[at, :] = add_low(own_ref[here, :], others[-1][there, :])
        return _

    lax.fori_loop(0, rows // 32, far_tile, 0)


def core_sum(own, *others):
    rows, width = own.shape[0] // 4, own.shape[1]
    shapes = [(rows // 2, width)] * 2 + [(rows, width)] * 3
    return pl.pallas_call(
        sum_kernel,
        in_specs=[pl.BlockSpec(memory_space=pltpu.VMEM)] * (1 + len(others)),
        out_specs=[pl.BlockSpec(memory_space=pltpu.VMEM)] * 5,
        out_shape=[jax.ShapeDtypeStruct(s, BF16) for s in shapes],
        compiler_params=pltpu.CompilerParams(vmem_limit_bytes=16 * 2**20),
        cost_estimate=NO_COST,
        name="core_sum",
    )(own, *others)


def way_kernel(ring_ref, *refs):
    pairs, outs = list(zip(refs[:-4:2], refs[1:-4:2])), refs[-4:]
    rows, width = outs[0].shape[0], pairs[0][0].shape[1]
    first = ring_ref[0] == 0
    blocks = [jnp.where(first, 1, 2), 3, jnp.where(first, 2, 1), 0]

    def tile(n, _):
        at = pl.ds(pl.multiple_of(n * 16, 16), 16)
        for block, out in zip(blocks, outs):
            here = pl.ds(pl.multiple_of(block * rows + n * 16, 16), 16)
            for k, (own_ref, other_ref) in enumerate(pairs):
                out[at, k * width : (k + 1) * width] = add_low(own_ref[here, :], other_ref[here, :])
        return _

    lax.fori_loop(0, rows // 16, tile, 0)


def core_sum_one_way(ring, *pairs):
    rows, width = pairs[0][0].shape[0] // 4, pairs[0][0].shape[1]
    vmem = pl.BlockSpec(memory_space=pltpu.VMEM)
    return pl.pallas_call(
        way_kernel,
        in_specs=[pl.BlockSpec(memory_space=pltpu.SMEM)] + [vmem] * (2 * len(pairs)),
        out_specs=[vmem] * 4,
        out_shape=[jax.ShapeDtypeStruct((rows, width * len(pairs)), BF16)] * 4,
        compiler_params=pltpu.CompilerParams(vmem_limit_bytes=24 * 2**20),
        cost_estimate=NO_COST,
        name="core_sum_one_way",
    )(ring, *(part for pair in pairs for part in pair))


def halves_kernel(after_0, after_1, before_0, before_1, into_right, into_left, right, left):
    right[0, 0] = add_low(after_0[0, 0], into_right[0])
    right[1, 0] = after_1[0, 0]
    left[0, 0] = before_0[0, 0]
    left[1, 0] = add_low(before_1[0, 0], into_left[0])


def fold_halves(after, before, into):
    shape = into[0].shape
    part = pl.BlockSpec((1, 1, *shape[1:]), lambda j: (0, j, 0, 0))
    block = pl.BlockSpec((1, *shape[1:]), lambda j: (j, 0, 0))
    return pl.pallas_call(
        halves_kernel,
        grid=(4,),
        in_specs=[part] * 4 + [block] * 2,
        out_specs=[pl.BlockSpec((2, 1, *shape[1:]), lambda j: (0, j, 0, 0))] * 2,
        out_shape=[jax.ShapeDtypeStruct((2, *shape), BF16)] * 2,
        compiler_params=pltpu.CompilerParams(dimension_semantics=("arbitrary",), vmem_limit_bytes=24 * 2**20),
        cost_estimate=NO_COST,
        name="fold_halves",
    )(*after, *before, *into)


def turn_kernel(count, me_ref, *refs):
    top, bottom, outs = refs[2 * count], refs[2 * count + 1], refs[2 * count + 2]
    step = pl.program_id(0)
    for half in range(2):
        blocks = [ref[...].reshape(outs.shape[2:]) for ref in refs[half * count : (half + 1) * count]]
        value = sum(block.astype(F32) for block in blocks).astype(BF16)

        @pl.when(step == 0)
        def _(value=value, half=half):
            (top, bottom)[half][...] = value

        @pl.when(step > 0)
        def _(value=value, half=half):
            outs[0, half] = value


def turn(me, parts):
    rows, width = parts[0][0][0].shape[-2:]

    def place_of(step, me_ref):
        ahead = jnp.where(step == 0, 2, jnp.where(step == 1, 0, jnp.where(step == 2, 1, 3)))
        return (me_ref[0] + ahead) % 4

    def spec(array, index):
        lead = len(array.shape) - 3
        return pl.BlockSpec(
            (1,) * (lead + 1) + (rows, width),
            lambda step, me_ref, index=index: (*index, place_of(step, me_ref), 0, 0),
        )

    arrays = [item for half in parts for item in half]
    return pl.pallas_call(
        functools.partial(turn_kernel, len(parts[0])),
        grid_spec=pltpu.PrefetchScalarGridSpec(
            num_scalar_prefetch=1,
            grid=(4,),
            in_specs=[spec(array, index) for array, index in arrays],
            out_specs=[pl.BlockSpec((rows, width), lambda step, me_ref: (0, 0))] * 2
            + [pl.BlockSpec((1, 2, rows, width), lambda step, me_ref: (jnp.maximum(step - 1, 0), 0, 0, 0))],
        ),
        out_shape=[jax.ShapeDtypeStruct((rows, width), BF16)] * 2
        + [jax.ShapeDtypeStruct((3, 2, rows, width), BF16)],
        compiler_params=pltpu.CompilerParams(dimension_semantics=("arbitrary",), vmem_limit_bytes=16 * 2**20),
        cost_estimate=NO_COST,
        name="turn",
    )(me, *(array for array, _ in arrays))


def parts_kernel(split, *refs):
    lefts, weight, outs = refs[:-3], refs[-3], refs[-2:]
    for n, out in enumerate(outs):
        left = lefts[0][n * split : (n + 1) * split, :] if len(lefts) == 1 else lefts[n][...]
        out[...] = dot_last(left, weight[...]).astype(BF16)


def token_parts(lefts, weight):
    vmem = pl.BlockSpec(memory_space=pltpu.VMEM)
    rows = sum(left.shape[0] for left in lefts) // 2
    return pl.pallas_call(
        functools.partial(parts_kernel, rows),
        in_specs=[vmem] * (len(lefts) + 1),
        out_specs=[vmem] * 2,
        out_shape=[jax.ShapeDtypeStruct((rows, weight.shape[0]), BF16)] * 2,
        compiler_params=pltpu.CompilerParams(vmem_limit_bytes=24 * 2**20),
        cost_estimate=cost(4 * rows * weight.shape[0] * weight.shape[1]),
        name="token_parts",
    )(*lefts, weight)


ONE_WAY = tuple((2 * i + c, 2 * ((i + 1 - 2 * c) % 4) + c) for i in range(4) for c in range(2))


def one_way(block):
    return lax.ppermute(block, GROUP, ONE_WAY)


def fold_kernel(behind_ref, before_ref, into_right_ref, into_left_ref, right_ref, left_ref):
    half = into_right_ref.shape[0]

    def tile(n, _):
        top = pl.ds(pl.multiple_of(n * 16, 16), 16)
        bottom = pl.ds(pl.multiple_of(half + n * 16, 16), 16)
        right_ref[top, :] = add_low(behind_ref[top, :], into_right_ref[top, :])
        right_ref[bottom, :] = behind_ref[bottom, :]
        left_ref[top, :] = before_ref[top, :]
        left_ref[bottom, :] = add_low(before_ref[bottom, :], into_left_ref[top, :])
        return _

    lax.fori_loop(0, half // 16, tile, 0)


def fold_tokens(behind, before, into, estimate=NO_COST):
    return pl.pallas_call(
        fold_kernel,
        in_specs=[pl.BlockSpec(memory_space=pltpu.VMEM)] * 4,
        out_specs=[pl.BlockSpec(memory_space=pltpu.VMEM)] * 2,
        out_shape=[jax.ShapeDtypeStruct(behind.shape, BF16)] * 2,
        compiler_params=pltpu.CompilerParams(vmem_limit_bytes=16 * 2**20),
        cost_estimate=estimate,
        name="fold_tokens",
    )(behind, before, *into)


def unshuffle_kernel(block, owned, value_ref, out):
    size = out.shape[1]
    order = lax.broadcasted_iota(jnp.int32, (1, size), 1)
    source = order // owned % 16 * block + order // (16 * owned) * owned + order % owned
    shuffle = jnp.where(lax.broadcasted_iota(jnp.int32, (size, size), 0) == source, 1.0, 0.0).astype(BF16)
    out[...] = dot_last(value_ref[...], shuffle)


def unshuffled(value, block, owned):
    return pl.pallas_call(
        functools.partial(unshuffle_kernel, block, owned),
        in_specs=[pl.BlockSpec(memory_space=pltpu.VMEM)],
        out_specs=pl.BlockSpec(memory_space=pltpu.VMEM),
        out_shape=jax.ShapeDtypeStruct(value.shape, F32),
        compiler_params=pltpu.CompilerParams(vmem_limit_bytes=24 * 2**20),
        cost_estimate=cost(2**34),
        name="unshuffled",
    )(value)


def split_up(value):
    high = lax.reduce_precision(value, 8, 7)
    middle = lax.reduce_precision(value - high, 8, 7)
    return [part.astype(BF16) for part in (high, middle, value - high - middle)]


def ahead_of(ring_ref, y, z):
    first = ring_ref[0] == 0
    return (jnp.where(first, y, z) - ring_ref[1] + 4) % 4, jnp.where(first, z, y)


def store_two_way(ring_ref, far_ref, near_refs, half, y, z, block, columns):
    ahead, then = ahead_of(ring_ref, y, z)

    @pl.when(ahead == 2)
    def _():
        far_ref[then, :, columns] = block

    for ref, place_ahead in zip(near_refs, (0, 1, 3)):

        @pl.when(ahead == place_ahead)
        def _(ref=ref):
            ref[half, then, :, columns] = block


def glu_grad_kernel(ring_ref, *refs):
    normed, grad, deltas, hidden, far_ref = refs[:5]
    y = pl.program_id(0)
    both = dot_rows(normed[...], deltas[...]).astype(BF16)
    down = dot_rows(grad[...], hidden[...]).astype(BF16)
    width = both.shape[1]
    for z in range(4):
        rows = slice(z * 64, z * 64 + 64)
        store_two_way(ring_ref, far_ref, refs[5:], 0, y, z, both[rows], slice(0, width))
        store_two_way(ring_ref, far_ref, refs[5:], 0, y, z, down[rows], slice(width, None))


def whole(value):
    return pl.BlockSpec(value.shape, lambda i: (0,) * value.ndim)


def in_hbm(value):
    return pltpu.with_memory_space_constraint(value, pltpu.HBM)


def glu_grads(ring, half, normed, grad, deltas, hidden):
    tokens, model = normed.shape
    width = deltas.shape[1] + hidden.shape[1]
    column = pl.BlockSpec((tokens, 256), lambda i: (0, 4 * half + i))
    shapes = [(4, 64, width)] + [(1, 4, 64, width)] * 3
    return pl.pallas_call(
        glu_grad_kernel,
        grid=(4,),
        in_specs=[pl.BlockSpec(memory_space=pltpu.SMEM), column, column, whole(deltas), whole(hidden)],
        out_specs=[pl.BlockSpec(s, lambda i, n=len(s): (0,) * n) for s in shapes],
        out_shape=[(pltpu.HBM if n == 1 else jax.ShapeDtypeStruct)(s, BF16) for n, s in enumerate(shapes)],
        compiler_params=pltpu.CompilerParams(
            dimension_semantics=("arbitrary",), vmem_limit_bytes=32 * 2**20
        ),
        cost_estimate=cost(tokens * model * width),
        name="glu_grads",
    )(ring, *map(in_hbm, (normed, grad, deltas, hidden)))


def weight_copies(copy, pieces, place_ref, targets):
    for n in range(4):
        for j in range(4):
            whole_ones = len(pieces) == 5 and n < 3
            piece = pieces[n] if whole_ones else pieces[(3 if len(pieces) == 5 else 2 * n) + j // 2]
            for h in range(2):
                rows = pl.ds(pl.multiple_of((h * 16 + place_ref[n * 4 + j]) * 64, 64), 64)
                for ref, at in targets:
                    copy(piece.at[j if whole_ones else j % 2, h, :, pl.ds(at, ref.shape[1])], ref.at[rows, :])


def glu_kernel(place_ref, *refs):
    weights, sources, grads, outs, scratch = refs[:8], refs[8:14], refs[14:16], refs[16:23], refs[23:]
    normed_out, grad_out, down_out, deltas_out, hidden_out, *back_outs = outs
    normed_ref, grad_ref, both_ref, down_ref, deltas_ref, hidden_ref, back_ref, sem = scratch
    copies = []

    def copy(source, target):
        copies.append(pltpu.make_async_copy(source, target, sem.at[len(copies)]))

    def gather(pieces, target):
        at = 0
        for piece in pieces:
            copy(piece, target.at[pl.ds(at, piece.shape[0]), :])
            at += piece.shape[0]

    def start(first, last):
        for each in copies[first:last]:
            each.start()

    def wait(first, last):
        for each in copies[first:last]:
            each.wait()

    width, rows = down_ref.shape[1], normed_ref.shape[0] // 2
    gather(sources, normed_ref)
    weight_copies(copy, weights, place_ref, [(both_ref, 0)])
    early = len(copies)
    gather(grads, grad_ref)
    weight_copies(copy, weights, place_ref, [(down_ref, both_ref.shape[1])])
    late = len(copies)
    start(0, late)
    copy(normed_ref, normed_out)
    copy(grad_ref, grad_out)
    copy(down_ref, down_out)
    whole_ones = len(copies)
    for half in range(2):
        at = pl.ds(half * rows, rows)
        copy(deltas_ref.at[at, :], deltas_out.at[at, :])
        copy(hidden_ref.at[at, :], hidden_out.at[at, :])
        copy(back_ref.at[at, :], back_outs[half])
    wait(0, early)
    start(late, late + 1)

    def one_half(half, carry):
        at = pl.ds(pl.multiple_of(half * rows, rows), rows)
        for n in range(0, width, 256):
            here, there = slice(n, n + 256), slice(width + n, width + n + 256)
            gate = dot(normed_ref[at, :], both_ref[:, here])
            up = dot(normed_ref[at, :], both_ref[:, there])
            sigma = jax.nn.sigmoid(gate)
            silu = gate * sigma
            hidden_ref[at, here] = (silu * up).astype(BF16)
            if n == 0:

                @pl.when(half == 0)
                def _():
                    wait(early, late)
                    start(late + 1, whole_ones)

            delta = dot(grad_ref[at, :], down_ref[:, here])
            slope = sigma * (1.0 + gate * (1.0 - sigma))
            deltas_ref[at, here] = (delta * up * slope).astype(BF16)
            deltas_ref[at, there] = (delta * silu).astype(BF16)
        for k in range(2):

            @pl.when(half == k)
            def _(first=whole_ones + 3 * k):
                start(first, first + 2)

        back_ref[at, :] = dot_last(deltas_ref[at, :], both_ref[...]).astype(BF16)
        for k in range(2):

            @pl.when(half == k)
            def _(last=whole_ones + 3 * k + 2):
                start(last, last + 1)

        return carry

    lax.fori_loop(0, 2, one_half, 0)
    wait(late, len(copies))


def glu_layer(weights, sources, grads, places):
    rows, model = sum(g.shape[0] for g in grads), grads[0].shape[1]
    padded = weights[0].shape[-1] // 3
    hbm, anywhere = pl.BlockSpec(memory_space=pltpu.HBM), pl.BlockSpec(memory_space=pl.ANY)
    shapes = [(rows, model), (rows, model), (model, padded)]
    near = [(rows, 2 * padded), (rows, padded)]
    scratch = [(rows, model), (rows, model), (model, 2 * padded), (model, padded), *near, (rows, model)]
    return pl.pallas_call(
        glu_kernel,
        in_specs=[pl.BlockSpec(memory_space=pltpu.SMEM)] + [anywhere] * 16,
        out_specs=[hbm] * 7,
        out_shape=[pltpu.HBM(s, BF16) for s in [*shapes, *near] + [(rows // 2, model)] * 2],
        scratch_shapes=[pltpu.VMEM(s, BF16) for s in scratch] + [pltpu.SemaphoreType.DMA((90,))],
        compiler_params=pltpu.CompilerParams(vmem_limit_bytes=34 * 2**20),
        cost_estimate=cost(10 * rows * model * padded),
        name="glu_layer",
    )(places, *weights, *sources, *grads)


def middle_kernel(own, right, left, gain, mixed, seed, branch, scale, delta_ref, out_ref):
    model = gain.shape[1]
    lane = lax.broadcasted_iota(jnp.int32, (16, LANES), 1)

    def tile(n, _):
        at = pl.ds(pl.multiple_of(n * 16, 16), 16)
        here = mixed[at, :]
        scale_two = inverse_rms(here)
        scaled = (own[at, :].astype(F32) + right[at, :].astype(F32) + left[at, :].astype(F32)) * gain[...]
        inner = jnp.mean(scaled * here, axis=-1, keepdims=True)
        delta = seed[at, :] + scale_two * scaled - here * (scale_two * scale_two * scale_two) * inner
        delta_ref[at, :] = delta
        low = delta.astype(BF16)
        out_ref[at, :model] = low
        inner = jnp.mean(low.astype(F32) * branch[at, :], axis=-1, keepdims=True)
        extra = jnp.zeros((16, LANES), F32)
        for first, value in ((0, scale[at, 0:1]), (3, inner)):
            for k in range(3):
                part = value.astype(BF16).astype(F32)
                extra = jnp.where(lane == first + k, part, extra)
                value = value - part
        out_ref[at, model:] = extra.astype(BF16)
        return _

    lax.fori_loop(0, mixed.shape[0] // 16, tile, 0)


def middle(own, right, left, gain, mixed, seed, branch, scale):
    rows, model = mixed.shape
    return pl.pallas_call(
        middle_kernel,
        in_specs=[pl.BlockSpec(memory_space=pltpu.VMEM)] * 8,
        out_specs=[pl.BlockSpec(memory_space=pltpu.VMEM)] * 2,
        out_shape=[jax.ShapeDtypeStruct((rows, model), F32), jax.ShapeDtypeStruct((rows, model + LANES), BF16)],
        compiler_params=pltpu.CompilerParams(vmem_limit_bytes=16 * 2**20),
        cost_estimate=NO_COST,
        name="middle",
    )(own, right, left, gain, mixed, seed, branch, scale)


def gates(p_i, p_f, bias):
    sig_i = jax.nn.sigmoid(p_i)
    inputs = (p_i * sig_i).astype(BF16).astype(F32)
    opened = jax.nn.sigmoid(p_f + bias)
    forget = (LOWER + (1.0 - LOWER) * opened).astype(BF16).astype(F32)
    return sig_i, inputs, opened, forget


def place(block_ref, t, m, span, micro):
    return pl.multiple_of(block_ref[t] * (span * micro) + m * span, span)


def mixer_kernel(span, micro, block_ref, place_ref, own_ref, *refs):
    pieces, halves = refs[:5], refs[5:7]
    rows_ref, channel_ref, mine_ref, other_refs, outs = *refs[7:10], refs[10:12], refs[12:17]
    tokens_ref, projected_ref, states_ref, in_ref, out_ref = refs[17:22]
    staged_ref, small_ref, picked_ref, u_ref, square_ref, sem = refs[22:]
    rows, model = tokens_ref.shape
    width = states_ref.shape[1]
    copies = []

    def copy(source, target):
        copies.append(pltpu.make_async_copy(source, target, sem.at[len(copies)]))

    for n, half in enumerate(halves):
        copy(half, tokens_ref.at[pl.ds(n * rows // 2, rows // 2), :])
    weight_copies(copy, pieces, place_ref, [(in_ref, 0), (small_ref, 3 * width)])
    for n in range(4):
        for j in range(4):
            piece = pieces[n] if n < 3 else pieces[3 + j // 2]
            for h in range(2):
                source = piece.at[j if n < 3 else j % 2, h, :, pl.ds(3 * width + LANES, width)]
                copy(source, staged_ref.at[h, place_ref[n * 4 + j]])
    for each in copies:
        each.start()
    for each in copies:
        each.wait()
    arrived = len(copies)

    def send(source, target):
        copy(source, target)
        copies[-1].start()

    send(in_ref, outs[3])

    pick = lax.broadcasted_iota(jnp.int32, (8, LANES), 0) == lax.broadcasted_iota(jnp.int32, (8, LANES), 1)
    pick = jnp.where(pick, 1.0, 0.0).astype(BF16)
    rows_ref[...] = dot_last(pick, small_ref[...])
    for n in range(16):
        start = pl.multiple_of(own_ref[0] + n * 64, 16)
        picked_ref[n * 16 : n * 16 + 16, :] = small_ref[pl.ds(start, 16), :]
    channel_ref[...] = dot_last(pick, picked_ref[...])

    def project(n, _):
        at = pl.ds(pl.multiple_of(n * 256, 256), 256)
        wide = tokens_ref[at, :].astype(F32)
        normed = (wide * inverse_rms(wide) * rows_ref[0:1, :]).astype(BF16)
        tokens_ref[at, :] = normed
        projected_ref[at, :] = dot(normed, in_ref[...])
        return _

    lax.fori_loop(0, rows // 256, project, 0)
    send(tokens_ref, outs[0])
    send(projected_ref, outs[1])

    gain, bias = channel_ref[1:2, :], channel_ref[3:4, :]
    row = lax.broadcasted_iota(jnp.int32, (span, width), 0) % 8
    for s, m in [(s, m) for s in range(2) for m in range(micro)]:
        carry = jnp.zeros((1, width), F32)
        for t in range(4):
            at = pl.ds(place(block_ref, 4 * s + t, m, span, micro), span)
            _, inputs, _, forget = gates(projected_ref[at, :width], projected_ref[at, width : 2 * width], bias)
            a, b = forget, (1.0 - forget) * inputs
            for d in (1, 2, 4):
                keep = row >= d
                a_before = jnp.where(keep, pltpu.roll(a, d, 0), 1.0)
                b_before = jnp.where(keep, pltpu.roll(b, d, 0), 0.0)
                b = a * b_before + b
                a = a * a_before
            parts = []
            for k in range(span // 8):
                now = a[k * 8 : k * 8 + 8] * carry + b[k * 8 : k * 8 + 8]
                carry = now[7:8]
                parts.append(now)
            states = jnp.concatenate(parts, axis=0)
            p_g = projected_ref[at, 2 * width :]
            states_ref[at, :] = states
            u_ref[at, :] = (states * gain * (p_g * jax.nn.sigmoid(p_g))).astype(BF16)
            square_ref[at, :] = jnp.broadcast_to(jnp.sum(states * states, axis=1, keepdims=True), (span, LANES))

    send(states_ref, outs[2])
    square = square_ref[...].astype(BF16)
    mine_ref[:, model:] = square[: rows // 2]
    for n, ref in enumerate(other_refs):
        ref[:, model:] = square[(2 + n) * rows // 4 : (3 + n) * rows // 4]
    for n in range(8):
        chunk = staged_ref[n // 4, :, n % 4 * 16 : n % 4 * 16 + 16, :].reshape(width, width)
        columns = slice(n * width, (n + 1) * width)
        out_ref[:, columns] = chunk
        part = dot(u_ref[...], chunk).astype(BF16)
        mine_ref[:, columns] = part[: rows // 2]
        for k, ref in enumerate(other_refs):
            ref[:, columns] = part[(2 + k) * rows // 4 : (3 + k) * rows // 4]
    send(out_ref, outs[4])
    for each in copies[arrived:]:
        each.wait()


def mixer_forward(blocks, places, own, pieces, halves, span, micro):
    rows, model = 2 * halves[0].shape[0], halves[0].shape[1]
    width = model // 8
    hbm, scalars = pl.BlockSpec(memory_space=pltpu.HBM), pl.BlockSpec(memory_space=pltpu.SMEM)
    small = [((8, model), F32), ((8, width), F32)]
    kept = [
        ((rows, model), BF16), ((rows, 3 * width), F32), ((rows, width), F32), ((model, 3 * width), BF16),
        ((width, model), BF16),
    ]
    parts = [((rows // n, model + LANES), BF16) for n in (2, 4, 4)]
    return pl.pallas_call(
        functools.partial(mixer_kernel, span, micro),
        in_specs=[scalars] * 3 + [pl.BlockSpec(memory_space=pl.ANY)] * 7,
        out_specs=[pl.BlockSpec(memory_space=pltpu.VMEM)] * 5 + [hbm] * 5,
        out_shape=[jax.ShapeDtypeStruct(*s) for s in small + parts] + [pltpu.HBM(*s) for s in kept],
        scratch_shapes=[pltpu.VMEM(*s) for s in kept]
        + [
            pltpu.VMEM((2, 16, 64, width), BF16),
            pltpu.VMEM((model, LANES), BF16),
            pltpu.VMEM((width, LANES), BF16),
            pltpu.VMEM((rows, width), BF16),
            pltpu.VMEM((rows, LANES), F32),
            pltpu.SemaphoreType.DMA((120,)),
        ],
        compiler_params=pltpu.CompilerParams(vmem_limit_bytes=26 * 2**20),
        cost_estimate=NO_COST,
        name="mixer_forward",
    )(blocks, places, own, *pieces, *halves)


def backward_kernel(span, micro, block_ref, ring_ref, values_ref, *refs):
    pieces, (projected, states, normed, out_shard), outs = refs[:6], refs[6:10], refs[10:16]
    low_ref, projected_ref, states_ref, normed_ref, out_ref, delta_ref, deltas_ref, gated_ref = refs[16:24]
    far_refs, near_refs, laid_ref, sem = refs[24:26], refs[26:29], refs[29], refs[30]
    rows, width = states_ref.shape
    model = normed_ref.shape[1]
    copies = []

    def copy(source, target):
        copies.append(pltpu.make_async_copy(source, target, sem.at[len(copies)]))
        copies[-1].start()

    at = 0
    for piece in pieces:
        copy(piece, low_ref.at[pl.ds(at, piece.shape[0]), :])
        at += piece.shape[0]
    copy(out_shard, out_ref)
    copy(projected, projected_ref)
    copy(states, states_ref)
    copy(normed, normed_ref)
    for each in copies[:7]:
        each.wait()
    delta_ref[...] = dot_last(low_ref[:, :model], out_ref[...])
    copies[7].wait()
    copies[8].wait()

    gain, bias = values_ref[1:2, :], values_ref[3:4, :]
    row = lax.broadcasted_iota(jnp.int32, (span, width), 0)
    row8 = row % 8
    for s, m in [(s, m) for s in range(2) for m in range(micro)]:
        carry = jnp.zeros((1, width), F32)
        for t in reversed(range(4)):
            at = pl.ds(place(block_ref, 4 * s + t, m, span, micro), span)
            p_i, p_g = projected_ref[at, :width], projected_ref[at, 2 * width :]
            sig_i, inputs, opened, forget = gates(p_i, projected_ref[at, width : 2 * width], bias)
            states, delta = states_ref[at, :], delta_ref[at, :]
            extra = low_ref[at, model:].astype(F32)
            scale = extra[:, 0:1] + extra[:, 1:2] + extra[:, 2:3]
            inner = extra[:, 3:4] + extra[:, 4:5] + extra[:, 5:6]
            sig_g = jax.nn.sigmoid(p_g)
            silu_g = p_g * sig_g
            hn = states * scale
            gated_ref[at, :] = (hn * gain * silu_g).astype(BF16)
            slope_g = sig_g * (1.0 + p_g * (1.0 - sig_g))
            deltas_ref[at, 2 * width :] = (delta * hn * gain * slope_g).astype(BF16)
            d_hn = delta * gain * silu_g
            d_states = scale * d_hn - states * (scale * scale * scale) * inner
            a, b = forget, forget * d_states
            for d in (1, 2, 4):
                keep = row8 < 8 - d
                a_after = jnp.where(keep, pltpu.roll(a, span - d, 0), 1.0)
                b_after = jnp.where(keep, pltpu.roll(b, span - d, 0), 0.0)
                b = a * b_after + b
                a = a * a_after
            parts = []
            for k in reversed(range(span // 8)):
                now = a[k * 8 : k * 8 + 8] * carry + b[k * 8 : k * 8 + 8]
                following = carry
                carry = now[0:1]
                up = pltpu.roll(now, 7, 0)
                parts.append(jnp.where(row8[:8] == 7, following, up))
            carried = d_states + jnp.concatenate(parts[::-1], axis=0)
            before = jnp.zeros((1, width), F32)
            if t > 0:
                tail = pl.multiple_of(place(block_ref, 4 * s + t - 1, m, span, micro) + span - 8, 8)
                before = states_ref[pl.ds(tail, 8), :][7:8]
            previous = jnp.where(row == 0, before, pltpu.roll(states, 1, 0))
            slope_i = sig_i * (1.0 + p_i * (1.0 - sig_i))
            deltas_ref[at, :width] = (carried * (1.0 - forget) * slope_i).astype(BF16)
            d_forget = carried * (previous - inputs) * (1.0 - LOWER) * opened * (1.0 - opened)
            deltas_ref[at, width : 2 * width] = d_forget.astype(BF16)

    copy(deltas_ref, outs[5])
    copies[9].wait()
    ones = jnp.ones((rows, LANES), BF16)
    bias_sum = dot_rows(deltas_ref[:, width : 2 * width], ones).astype(BF16)
    laid_ref[:, model:] = bias_sum
    laid_ref[:, :model] = dot_rows(gated_ref[...], low_ref[:, :model]).astype(BF16)

    for half in range(2):
        for y in range(4):
            features = slice((half * 4 + y) * 256, (half * 4 + y + 1) * 256)
            part = dot_rows(normed_ref[:, features], deltas_ref[...]).astype(BF16)
            first = half * model // 2
            for z in range(4):
                here = slice(y * 64 + z * 16, y * 64 + z * 16 + 16)
                laid = [laid_ref[here, first + n * width : first + (n + 1) * width] for n in range(4)]
                bias_part = [laid_ref[here, model:]] * 4
                for value, columns in (
                    (part[z * 64 : z * 64 + 64], slice(0, 3 * width)),
                    (jnp.concatenate(laid, axis=0), slice(3 * width, 4 * width)),
                    (jnp.concatenate(bias_part, axis=0), slice(4 * width, None)),
                ):
                    store_two_way(ring_ref, far_refs[half], near_refs, half, y, z, value, columns)
        copy(far_refs[half], outs[half])
    for ref, out in zip(near_refs, outs[2:5]):
        copy(ref, out)
    for each in copies[10:]:
        each.wait()


def mixer_backward(blocks, ring, values, pieces, projected, states, normed, out_shard, span, micro):
    rows, width = states.shape
    model = normed.shape[1]
    total_width = 4 * width + LANES
    hbm, scalars = pl.BlockSpec(memory_space=pltpu.HBM), pl.BlockSpec(memory_space=pltpu.SMEM)
    ring_shapes = [(4, 64, total_width)] * 2 + [(2, 4, 64, total_width)] * 3
    return pl.pallas_call(
        functools.partial(backward_kernel, span, micro),
        in_specs=[scalars, scalars, pl.BlockSpec(memory_space=pltpu.VMEM)] + [pl.BlockSpec(memory_space=pl.ANY)] * 10,
        out_specs=[hbm] * 6,
        out_shape=[pltpu.HBM(s, BF16) for s in ring_shapes + [(rows, 3 * width)]],
        scratch_shapes=[
            pltpu.VMEM((rows, model + LANES), BF16),
            pltpu.VMEM((rows, 3 * width), F32),
            pltpu.VMEM((rows, width), F32),
            pltpu.VMEM((rows, model), BF16),
            pltpu.VMEM((width, model), BF16),
            pltpu.VMEM((rows, width), F32),
            pltpu.VMEM((rows, 3 * width), BF16),
            pltpu.VMEM((rows, width), BF16),
            *[pltpu.VMEM(s, BF16) for s in ring_shapes],
            pltpu.VMEM((width, model + LANES), BF16),
            pltpu.SemaphoreType.DMA((16,)),
        ],
        compiler_params=pltpu.CompilerParams(vmem_limit_bytes=28 * 2**20),
        cost_estimate=cost(20 * rows * model * width),
        name="mixer_backward",
    )(blocks, ring, values, *pieces, *map(in_hbm, (projected, states, normed, out_shard)))


def shards(
    tokens, cotangent, lengths, in_weight, out_weight, norm_gains, forget_bias, gate_weight, up_weight, down_weight
):
    micro, _, span, model = tokens.shape
    own_rows = micro * span
    owned = in_weight.shape[1]
    rows = 4 * owned
    width = model // 8
    glu = gate_weight.shape[2]
    half = glu // 2
    padded = -(-half // LANES) * LANES
    xh, xl, core, y, z = (lax.axis_index(a) for a in ("xh", "xl", "c", "y", "z"))
    chip = xh * 2 + xl
    ahead = (jnp.arange(4) - chip) % 4
    nth = jnp.where(ahead == 3, 1, jnp.where(ahead == 0, 0, ahead + 1)).astype(jnp.int32)
    blocks = (nth[:, None] + jnp.where(jnp.arange(2)[None, :] == core, 0, 4)).reshape(8).astype(jnp.int32)
    offsets = jnp.array(OFFSETS)
    by_y = ((y + offsets) % 4 * 4)[:, None] + ((z + offsets) % 4)[None, :]
    places = jnp.where(core == 0, by_y, by_y.T).reshape(16).astype(jnp.int32)
    ring = jnp.stack([core, jnp.where(core == 0, y, z)]).astype(jnp.int32)
    own_start = (xh * (model // 2) + (xl * 2 + core) * owned).astype(jnp.int32).reshape(1)

    def halves(weight):
        low = jnp.pad(weight[0, :, :half], ((0, 0), (0, padded - half)))
        high = jnp.pad(weight[0, :, half:], ((0, 0), (0, padded - half)))
        return low, high

    low, high = (jnp.concatenate(h, axis=1) for h in zip(*map(halves, (gate_weight, up_weight, down_weight))))
    glu_sent = jnp.where(xh == 0, high, low)
    glu_arrived = lax.ppermute(glu_sent, "xh", SWAP)
    glu_kept = jnp.where(xh == 0, low, high)

    own_tokens = tokens.reshape(own_rows, model)
    positions = (xl * 2 + core) * span + jnp.arange(span)
    keep = (positions[None, :] < lengths).astype(F32).reshape(-1, 1)
    seed = cotangent.reshape(own_rows, model).astype(F32) * keep

    w_in, w_out = in_weight[0], out_weight[0]
    order = jnp.arange(model // 2)
    source = (order // owned % 16) * rows + (order // (16 * owned)) * owned + order % owned
    shuffle = (jnp.arange(model // 2)[:, None] == source[None, :]).astype(BF16)
    by_shard = dot(w_in.reshape(owned * 6, model // 2), shuffle).astype(BF16)
    by_shard = by_shard.reshape(owned, 3, 2, 4, width).transpose(2, 3, 0, 1, 4).reshape(8, owned, 3 * width)
    small = jnp.concatenate([norm_gains[0], forget_bias[0][:, None]], axis=1)
    small = jnp.pad(small, ((0, 0), (0, LANES - 4)))
    sent = jnp.concatenate([by_shard, jnp.broadcast_to(small[None], (8, owned, LANES))], axis=2)
    sent = held(sent, glu_sent)
    in_rows = lax.all_to_all(sent, GROUP, 0, 0, tiled=True).reshape(2, rows, -1)
    out_rows = w_out.reshape(owned, 2, 4, width).transpose(1, 2, 0, 3).reshape(2, rows, width)
    mixer_block = jnp.concatenate([in_rows, out_rows], axis=2)
    glu_parts = jnp.where(xh == 0, glu_kept, glu_arrived), jnp.where(xh == 0, glu_arrived, glu_kept)
    glu_block = jnp.stack(glu_parts)
    mixer_width = mixer_block.shape[2]

    along_z, along_y = (PLANE, "z"), (PLANE, "y")
    block = jnp.concatenate([mixer_block, glu_block], axis=2)
    near = both_ways(block, along_z)
    tokens_near = both_ways(held(own_tokens, block), CHIPS)
    near = in_turn(*near, *tokens_near)
    near, tokens_near = near[:2], near[2:]
    far = far_halves(*near, along_z)
    tokens_far = far_halves(*tokens_near, CHIPS)
    far, tokens_far = in_turn(far, tokens_far)
    pieces = [block, *near, jnp.concatenate(far, axis=0)]
    tokens_own = jnp.concatenate([own_tokens, *tokens_near, *tokens_far], axis=0)
    tokens_other = beside(tokens_own)
    mixer_block = jnp.stack([p[:, :, :mixer_width] for p in pieces])
    grad_low = held(seed.astype(BF16), mixer_block)
    grad_near = both_ways(grad_low, CHIPS)
    mixer_near = held(both_ways(mixer_block, along_y), *grad_near)
    mixer_far = far_halves(*mixer_near, along_y)
    grad_far = far_halves(*held(grad_near, *mixer_near), CHIPS)
    glu_block = [jnp.stack([p[:, :, mixer_width:] for p in pieces[at : at + 2]]) for at in (0, 2)]
    glu_block = held(glu_block, mixer_near)
    mixer_pieces = held([mixer_block, *mixer_near, *mixer_far], *glu_block, *grad_far)
    grad_own = jnp.concatenate([grad_low, *grad_near, *grad_far], axis=0)
    glu_near_0 = both_ways(glu_block[0], along_y)

    row_values, channel_values, mine, other_near, other_far, normed, projected, states, in_shard, out_shard = mixer_forward(
        blocks, places, own_start, mixer_pieces, (tokens_own, tokens_other), span, micro
    )
    gain_one, gain_two = row_values[0], row_values[2]
    top, bottom, own, before, behind = core_sum(held(mine, *glu_near_0), beside(other_near), beside(other_far))
    into = send_far(top, bottom, CHIPS)
    right, left = fold_tokens(behind, before, into)
    glu_near_1 = both_ways(held(glu_block[1], top), along_y)
    grad_other = beside(held(grad_own, top, bottom))
    right, left = held((right, left), grad_other)
    into = send_near(right, left, CHIPS)
    mix_sum = total(own, into)
    branch_mix, square_sum = mix_sum[:, :model], mix_sum[:, model : model + 1]
    current = own_tokens.astype(F32)
    scale_state = lax.rsqrt(square_sum / model + EPS)
    mixed = current + scale_state * branch_mix

    scale_two = inverse_rms(mixed)
    own = (mixed * scale_two * gain_two).astype(BF16)
    near, other = both_ways(own, CHIPS), beside(own)
    glu_far = send_far(*held((glu_near_0[0], glu_near_1[1]), own, glu_near_1[0]), along_y)
    *near, other = in_turn(*near, other)
    far = far_halves(*near, CHIPS)
    sides = jnp.concatenate(near, axis=0)
    others = beside(held(sides, *far))
    glu_pieces = [*glu_block, *(near[way] for way in (0, 1) for near in (glu_near_0, glu_near_1)), *held(glu_far, sides)]
    far = jnp.concatenate(far, axis=0)
    token_rows = [own, sides, far, other, others, beside(far)]

    normed_two, grad_all, down_shard, deltas, hidden, back_own, back_other = glu_layer(
        glu_pieces, token_rows, [grad_own, grad_other], places
    )
    top, bottom, own, before, behind = core_sum(back_own, beside(back_other))
    deltas, hidden, normed_two, grad_all = held((deltas, hidden, normed_two, grad_all), top)
    arrived = send_far(top, bottom, CHIPS)
    glu_far_0, *glu_near_0 = glu_grads(ring, 0, normed_two, grad_all, deltas, hidden)
    arrived, glu_far_0 = in_turn(arrived, glu_far_0)
    right, left = fold_tokens(behind, before, arrived)
    deltas, hidden, normed_two, grad_all = held((deltas, hidden, normed_two, grad_all), right, left)
    arrived = send_near(right, left, CHIPS)
    glu_far_1, *glu_near_1 = glu_grads(ring, 1, normed_two, grad_all, deltas, hidden)
    glu_far = send_far(glu_far_0, glu_far_1, along_y)
    arrived, glu_far_0, glu_far_1 = in_turn(arrived, glu_far_0, glu_far_1)

    mixed_delta, extended = middle(own, *arrived, gain_two[None], mixed, seed, branch_mix, scale_state)
    near, other = both_ways(extended, CHIPS), beside(extended)
    branch_own, branch_other = token_parts([held(hidden, extended)], down_shard)
    *near, other, branch_other = in_turn(*near, other, branch_other)
    far = far_halves(*near, CHIPS)
    sides = jnp.concatenate(near, axis=0)
    others = beside(sides)
    branch_other = beside(held(branch_other, sides))
    glu_right, glu_left = fold_halves(
        (glu_near_0[1], glu_near_1[1]), (glu_near_0[2], glu_near_1[2]), held(glu_far, sides)
    )
    far, glu_right, glu_left = in_turn(far, glu_right, glu_left)
    glu_near = send_near(glu_right, glu_left, along_y)
    far = jnp.concatenate(far, axis=0)
    far_other = beside(far)
    branch_top, branch_bottom, branch, branch_before, branch_behind = core_sum(branch_own, held(branch_other, far))
    branch_far = send_far(branch_top, branch_bottom, CHIPS)
    pieces = held([extended, sides, far, other, others, far_other], branch_top)
    mix_far_0, mix_far_1, mix_own, mix_after, mix_before, deltas_in = mixer_backward(
        blocks, ring, channel_values, pieces, projected, states, normed, out_shard, span, micro
    )
    me = jnp.where(core == 0, z, y).astype(jnp.int32).reshape(1)

    def folded(after, before, into, estimate=NO_COST):
        shape = after.shape
        after, before = after.reshape(-1, shape[-1]), before.reshape(-1, shape[-1])
        into = [part.reshape(-1, shape[-1]) for part in into]
        return [part.reshape(shape) for part in fold_tokens(after, before, into, estimate)]

    mix_far_0, mix_far_1 = held((mix_far_0, mix_far_1), *glu_near, *branch_far)
    mix_far = send_far(mix_far_0, mix_far_1, along_y)
    branch_far, glu_near = held((branch_far, glu_near), mix_far_0, mix_far_1)
    branch_right, branch_left = fold_tokens(branch_behind, branch_before, branch_far)
    branch_near = send_near(branch_right, branch_left, CHIPS)
    glu_top, glu_bottom, glu_last = turn(
        me, [[(own, (0,)), (glu_near[0], (n,)), (glu_near[1], (n,))] for n, own in ((0, glu_near_0[0]), (1, glu_near_1[0]))]
    )
    mix_far = held(mix_far, glu_top, branch_right)
    mix_right, mix_left = folded(mix_after, mix_before, mix_far)
    mix_near = send_near(mix_right, mix_left, along_y)
    branch_sum = total(branch, held(branch_near, mix_right, mix_left))
    glu_far = send_far(*held((glu_top, glu_bottom), branch_sum), along_z)
    first_own, first_other = token_parts([held(deltas_in, mix_right, mix_left)], in_shard)
    glu_right, glu_left = folded(glu_last[1], glu_last[2], glu_far)
    mix_near = held(mix_near, first_own, glu_right)
    mix_top, mix_bottom, mix_last = turn(me, [[(part, (n,)) for part in (mix_own, *mix_near)] for n in range(2)])
    mix_far = send_far(mix_top, mix_bottom, along_z)
    glu_near = send_near(*held((glu_right, glu_left), mix_top), along_z)
    first_other = beside(held(first_other, mix_top))
    top, bottom, first, before, behind = core_sum(first_own, first_other)
    mix_right, mix_left = folded(mix_last[1], mix_last[2], held(mix_far, top), cost(2**32))
    mix_near = send_near(mix_right, mix_left, along_z)
    first_far = send_far(*held((top, bottom), mix_right, mix_left), CHIPS)
    glu_sum = total(glu_last[0], held(glu_near, mix_right, mix_left))
    here = held(glu_sum, *first_far)[:, :, : 2 * padded]
    last_part = [jnp.sum(part[:, : 2 * padded].astype(F32) * here[n], axis=-1) for n, part in enumerate(glu_parts)]
    last_part = jnp.stack(last_part).reshape(8, owned, 1)
    lane = jnp.arange(LANES)
    last_part = sum(jnp.where(lane == n, part, 0) for n, part in enumerate(split_up(last_part))).astype(BF16)
    mix_near = held(mix_near, last_part)
    mixer = total(mix_last[0], mix_near)
    first_far = held(first_far, mixer)
    right, left = fold_tokens(behind, before, first_far)
    first_sum = total(first, send_near(right, left, CHIPS))

    in_sum = mixer[..., : 3 * width].astype(BF16).reshape(8, owned, 3 * width)
    in_sum = lax.all_to_all(jnp.concatenate([in_sum, last_part], axis=-1), GROUP, 0, 0, tiled=True)
    in_sum = held(in_sum, right, left)
    gains_last = jnp.sum(in_sum[:, :, 3 * width : 3 * width + 3].astype(F32), axis=(0, 2))
    in_sum = in_sum[:, :, : 3 * width]
    in_sum = in_sum.reshape(2, 4, owned, 3, width).transpose(2, 3, 0, 1, 4).reshape(owned * 6, model // 2)
    in_grad = unshuffled(in_sum, rows, owned).reshape(owned, 3 * model)
    out_grad = mixer[..., 3 * width : 4 * width].reshape(2, 4, owned, width).transpose(2, 0, 1, 3).reshape(owned, model)
    bias_grad = mixer[0, :owned, 4 * width]

    first_delta = first_sum
    scaled_one = first_delta * gain_one
    current = held(own_tokens, right, left).astype(F32)
    scale_one = inverse_rms(current)
    token_grad = (
        mixed_delta
        + scale_one * scaled_one
        - current * (scale_one * scale_one * scale_one) * jnp.mean(scaled_one * current, axis=-1, keepdims=True)
    )

    activations = mixed + branch_sum

    kept = lax.dynamic_index_in_dim(glu_sum, xh, 0, keepdims=False)
    arrived = lax.dynamic_index_in_dim(glu_sum, 1 - xh, 0, keepdims=False)
    arrived = arrived.astype(BF16)
    arrived = held(lax.ppermute(arrived, "xh", SWAP), right, left).astype(F32)
    low, high = jnp.where(xh == 0, kept, arrived), jnp.where(xh == 0, arrived, kept)
    gate_grad, up_grad, down_grad = (
        jnp.concatenate([low[:, at : at + half], high[:, at : at + half]], axis=1) for at in (0, padded, 2 * padded)
    )

    own_gains = norm_gains[0].astype(F32)
    gains_first = jnp.sum(w_in.astype(F32) * in_grad, axis=1) / own_gains[:, 0]
    gains_mid = jnp.sum(w_out.astype(F32) * out_grad, axis=1) / own_gains[:, 1]
    gains_last = gains_last / own_gains[:, 2]
    gains_grad = jnp.stack([gains_first, gains_mid, gains_last], axis=1)

    shape = tokens.shape
    return (
        activations.reshape(shape),
        token_grad.reshape(shape),
        in_grad[None],
        out_grad[None],
        gains_grad[None],
        bias_grad[None],
        gate_grad[None],
        up_grad[None],
        down_grad[None],
    )


def solution(mesh):
    fine = Mesh(mesh.devices.reshape(2, 4, 4, 2, 2), DP + TENSOR)
    token = P(None, DP, TENSOR, None)
    mixer = P(None, DP + TENSOR, None)
    vector = P(None, DP + TENSOR)
    glu = P(None, DP, TENSOR)
    return jax.shard_map(
        shards,
        mesh=fine,
        in_specs=(token, token, P(None, DP), mixer, mixer, mixer, vector, glu, glu, glu),
        out_specs=(token, token, mixer, mixer, mixer, vector, glu, glu, glu),
        check_vma=False,
    )
```
